32 devices in a mesh: energy: 8 (over y, x, core), cell: 4 (over z).
Axes of the slice: x: 2, y: 2, z: 4, core: 2. Of those that a mesh axis runs over, the one named last changes fastest.
Arguments:
- retarded_diag: bfloat16 [2, 16, 16, 256, 256], P(None, 'energy', 'cell'), may hold values from -0.375 to 0.375
- retarded_lower: bfloat16 [2, 16, 16, 256, 256], P(None, 'energy', 'cell'), may hold values from -0.375 to 0.375
- retarded_upper: bfloat16 [2, 16, 16, 256, 256], P(None, 'energy', 'cell'), may hold values from -0.375 to 0.375
- sigma_lesser: bfloat16 [2, 16, 16, 256, 256], P(None, 'energy', 'cell'), may hold values from -6 to 6
- screened: bfloat16 [2, 16, 32], P(None, 'cell'), may hold values from -1 to 1
- kept: int32 [16, 8], P('cell'), may hold values from 0 to 15, as said below
- kept_count: int32 [16], P('cell'), may hold values from 1 to 8, as said below
Outputs:
- sigma_new: bfloat16 [2, 16, 16, 8, 4096], P(None, 'energy', 'cell')
The draws below stay inside these ranges and needn't reach their ends.
Inputs may be any that keep to these rules, and one draw needn't show every extreme that they name: `kept`: each row holds 8 different sub-block numbers. `kept_count`: some cell has 8 live slots and some other cell 1.
All inputs are finite; a program needn't handle non-finite values.
Results may differ from the reference program's by a relative error of at most 0.0057.
Values may be sent and summed in bfloat16 or wider, within the bound.
No kernel may reach another device: no remote copies, remote signals or barrier semaphores. Data moves between devices by JAX's collectives and lax.ppermute only.
A program may use at most 128 MiB of HBM per device.

```python
import jax
import jax.numpy as jnp
from jax import lax

ORB = 256
SUB = 64
KMAX = 8
ENERGIES = 16
CELLS = 16


def draw_kept(key, part):
    block_count = ORB // SUB * (ORB // SUB)
    key_scores = jax.random.fold_in(key, 101)
    scores = jax.random.randint(key_scores, (CELLS, block_count), 0, 1 << 20) * block_count
    scores = scores + jnp.arange(block_count, dtype=jnp.int32)[None, :]
    return lax.top_k(scores, KMAX)[1].astype(jnp.int32)


def draw_kept_count(key, part):
    key_counts = jax.random.fold_in(key, 202)
    key_full = jax.random.fold_in(key, 303)
    key_empty = jax.random.fold_in(key, 404)
    counts = jax.random.randint(key_counts, (CELLS,), 1, KMAX + 1)
    fullest = jax.random.randint(key_full, (), 0, CELLS)
    emptiest = (fullest + 1 + jax.random.randint(key_empty, (), 0, CELLS - 1)) % CELLS
    position = jnp.arange(CELLS, dtype=jnp.int32)
    counts = jnp.where(position == emptiest, 1, counts)
    counts = jnp.where(position == fullest, KMAX, counts)
    return counts.astype(jnp.int32)


def level_of(key, dims, pieces, smallest, top_value):
    def one(dim, blocks):
        heights = jax.random.uniform(jax.random.fold_in(jax.random.fold_in(key, 6), dim), (blocks,), jnp.float32, smallest / len(pieces), top_value / len(pieces))
        return jnp.repeat(jnp.exp(heights), dims[dim] // blocks).reshape((-1,) + (1,) * (len(dims) - dim - 1))

    factor_of = one(*pieces[0])
    for cut in pieces[1:]:
        factor_of = factor_of * one(*cut)
    return factor_of


def scatter_about(own_key, shape, scale, limit, split=(), kind=jnp.bfloat16):
    factor_of = level_of(own_key, shape, split, -0.22, 0.18) if split else 1.0
    values = jax.random.normal(own_key, shape, jnp.float32) * scale * factor_of
    return jnp.minimum(jnp.maximum(values, -limit), limit).astype(kind)


def setup_inputs(seed: int = 0) -> dict:
    key_list = jax.random.split(jax.random.key(seed), 8)
    retarded_diag = scatter_about(key_list[0], (2, ENERGIES, CELLS, ORB, ORB), ORB ** -0.5, 0.375, ((1, 8), (2, 4)))
    retarded_lower = scatter_about(key_list[1], (2, ENERGIES, CELLS, ORB, ORB), ORB ** -0.5, 0.375, ((1, 8), (2, 4)))
    retarded_upper = scatter_about(key_list[2], (2, ENERGIES, CELLS, ORB, ORB), ORB ** -0.5, 0.375, ((1, 8), (2, 4)))
    sigma_lesser = scatter_about(key_list[3], (2, ENERGIES, CELLS, ORB, ORB), 1.0, 6.0, ((1, 8), (2, 4)))
    screened = scatter_about(key_list[4], (2, CELLS, 2 * ENERGIES), (2 * ENERGIES) ** -0.5, 1.0, ((1, 4),))
    kept = draw_kept(jax.random.fold_in(key_list[7], 71), 0)
    kept_count = draw_kept_count(jax.random.fold_in(key_list[7], 71), 0)
    return {"retarded_diag": retarded_diag, "retarded_lower": retarded_lower, "retarded_upper": retarded_upper, "sigma_lesser": sigma_lesser, "screened": screened, "kept": kept, "kept_count": kept_count}


def batched(left_side, right_side):
    return jnp.einsum("cij,cjk->cik", left_side.astype(jnp.float32), right_side.astype(jnp.float32))


def batched_t(left_side, right_side):
    return jnp.einsum("cij,ckj->cik", left_side.astype(jnp.float32), right_side.astype(jnp.float32))


def sandwich(factor, middle):
    inner_r = (batched(factor[0], middle[0]) - batched(factor[1], middle[1])).astype(jnp.bfloat16)
    inner_i = (batched(factor[0], middle[1]) + batched(factor[1], middle[0])).astype(jnp.bfloat16)
    outer_r = batched_t(inner_r, factor[0]) + batched_t(inner_i, factor[1])
    outer_i = batched_t(inner_i, factor[0]) - batched_t(inner_r, factor[1])
    return outer_r, outer_i


def lesser_one(inputs):
    retarded_diag, retarded_lower, retarded_upper, sigma_lesser = inputs
    zero_cell = jnp.zeros_like(sigma_lesser[:, :1])
    prev_cell = jnp.concatenate([zero_cell, sigma_lesser[:, :-1]], axis=1)
    next_cell = jnp.concatenate([sigma_lesser[:, 1:], zero_cell], axis=1)
    first_r, first_i = sandwich(retarded_diag, sigma_lesser)
    second_r, second_i = sandwich(retarded_lower, prev_cell)
    third_r, third_i = sandwich(retarded_upper, next_cell)
    real_part = first_r + second_r + third_r
    imag_part = first_i + second_i + third_i
    return jnp.stack([real_part, imag_part]).astype(jnp.bfloat16)


def select_blocks(blocks, kept, sub_size):
    per_side = blocks.shape[3]
    row_pick = (kept // per_side)[None, None, :, :, None, None]
    col_pick = (kept % per_side)[None, None, :, :, None, None, None]
    row_blocks = jnp.take_along_axis(blocks, row_pick, axis=3)
    shaped = row_blocks.reshape(row_blocks.shape[:5] + (per_side, sub_size))
    picked = jnp.take_along_axis(shaped, col_pick, axis=5)
    return picked.reshape(picked.shape[:4] + (picked.shape[4] * sub_size,))


def toeplitz(screened):
    energy_count = screened.shape[2] // 2
    position = jnp.arange(energy_count, dtype=jnp.int32)
    offsets = position[:, None] - position[None, :] + energy_count - 1
    return jnp.take(screened, offsets, axis=2)


def convolve(kernel, chosen):
    kernel_r = kernel[0].astype(jnp.float32)
    kernel_i = kernel[1].astype(jnp.float32)
    chosen_r = chosen[0].astype(jnp.float32)
    chosen_i = chosen[1].astype(jnp.float32)
    real_part = jnp.einsum("cef,fckn->eckn", kernel_r, chosen_r) - jnp.einsum("cef,fckn->eckn", kernel_i, chosen_i)
    imag_part = jnp.einsum("cef,fckn->eckn", kernel_r, chosen_i) + jnp.einsum("cef,fckn->eckn", kernel_i, chosen_r)
    return jnp.stack([real_part, imag_part]).astype(jnp.bfloat16)


def reference(retarded_diag, retarded_lower, retarded_upper, sigma_lesser, screened, kept, kept_count):
    inputs = tuple(jnp.moveaxis(item, 1, 0) for item in (retarded_diag, retarded_lower, retarded_upper, sigma_lesser))
    lesser = jnp.moveaxis(lax.map(lesser_one, inputs), 0, 1)
    per_side = ORB // SUB
    blocks = lesser.reshape(2, ENERGIES, CELLS, per_side, SUB, ORB)
    chosen = select_blocks(blocks, kept, SUB)
    live_slots = (jnp.arange(KMAX, dtype=jnp.int32)[None, :] < kept_count[:, None]).astype(jnp.bfloat16)
    chosen = chosen * live_slots[None, None, :, :, None]
    return convolve(toeplitz(screened), chosen)
```

```python
from functools import partial

import jax
import jax.numpy as jnp
from jax import lax
from jax.experimental import pallas as pl
from jax.experimental.pallas import tpu as pltpu
from jax.sharding import PartitionSpec as P

SUB = 64
LANES = 2 * SUB
PAIRS = SUB // 2
STEP = 8


def packing_order(cell_count):
    interior = list(range(1, cell_count - 1))
    return interior + [0, cell_count - 1] if cell_count > 1 else [0]


def slot_base(count_ref, order, position):
    base = jnp.int32(0)
    for place, cell in enumerate(order[:-1]):
        base = base + jnp.where(place < position, count_ref[cell], 0)
    return base


def inner_products(factor, middle_r, middle_i, out_ref):
    row = jnp.concatenate([factor[0, 0, 0], factor[1, 0, 0]], axis=1)
    real_part = jnp.dot(
        row, jnp.concatenate([middle_r, -middle_i], axis=0), preferred_element_type=jnp.float32
    )
    out_ref[0] = real_part.astype(jnp.bfloat16)
    imag_part = jnp.dot(
        row, jnp.concatenate([middle_i, middle_r], axis=0), preferred_element_type=jnp.float32
    )
    out_ref[1] = imag_part.astype(jnp.bfloat16)


def paired_rows(product_ref, slot, group):
    def rows(half, odd):
        start = half * SUB + group * 2 * STEP + odd
        return product_ref[slot, pl.ds(start, STEP, stride=2), :]

    left = lax.broadcasted_iota(jnp.int32, (STEP, LANES), 1) < SUB
    top_even, top_odd = rows(0, 0), rows(0, 1)
    low_even, low_odd = rows(1, 0), rows(1, 1)
    real_part = jnp.where(left, top_even, low_odd) + pltpu.roll(
        jnp.where(left, top_odd, low_even), SUB, 1
    )
    imag_part = jnp.where(left, low_even, -top_odd) + pltpu.roll(
        jnp.where(left, low_odd, -top_even), SUB, 1
    )
    return real_part, imag_part


def lesser_kernel(order, first, devices, kept_ref, count_ref, *refs):
    if first:
        diag, lower, upper, own, prev, after, out_ref, inner, product, staged = refs
        prev_r, prev_i = prev[0, 0, 0], prev[1, 0, 0]
        next_r, next_i = after[0, 0, 0], after[1, 0, 0]
    else:
        (diag, lower, upper, own, near, low, high, earlier, out_ref, inner, product, staged, sides) = refs
    place, energy = pl.program_id(0), pl.program_id(1)
    energies = pl.num_programs(1)
    cell_count = len(order)
    if first:
        position = place
        cell = place + 1
    else:
        position = place + cell_count - 2
        cell = place * (cell_count - 1)

        @pl.when((place == 0) & (energy == 0))
        def _():
            out_ref[...] = earlier[...]

        @pl.when(place == 0)
        def _():
            sides[0] = low[:, 0, 0]
            sides[1] = near[:, 0, 0]

        @pl.when(place != 0)
        def _():
            sides[0] = near[:, 0, 0]
            sides[1] = high[:, 0, 0]

        prev_r, prev_i = sides[0, 0], sides[0, 1]
        next_r, next_i = sides[1, 0], sides[1, 1]
    base = slot_base(count_ref, order, position)
    inner_products(diag, own[0, 0, 0], own[1, 0, 0], inner.at[0])
    inner_products(lower, prev_r, prev_i, inner.at[1])
    inner_products(upper, next_r, next_i, inner.at[2])
    slots = kept_ref.shape[1]
    per_side = diag.shape[3] // SUB
    tile_rows = out_ref.shape[2]
    share = PAIRS // devices
    for slot in range(slots):
        number = kept_ref[cell, slot]
        top = pl.multiple_of((number // per_side) * SUB, SUB)
        side = pl.multiple_of((number % per_side) * SUB, SUB)
        left_parts = []
        right_parts = []
        for term, factor in enumerate((diag, lower, upper)):
            size = inner.shape[-1]
            left_parts.append(inner[term, :, pl.ds(top, SUB), :].reshape(LANES, size))
            right_parts.append(factor[:, 0, 0, pl.ds(side, SUB), :].reshape(LANES, size))
        product[slot] = lax.dot_general(
            jnp.concatenate(left_parts, axis=1),
            jnp.concatenate(right_parts, axis=1),
            (((1,), (1,)), ((), ())),
            preferred_element_type=jnp.float32,
        )
        for group in range(PAIRS // STEP):
            pair = paired_rows(product, slot, group)
            device = (group * STEP) % devices
            for part in range(2):
                start = device * tile_rows + (energy * 2 + part) * share + group * STEP // devices
                staged[slot, pl.ds(start, STEP, stride=tile_rows), :] = pair[part]

    @pl.when(energy == energies - 1)
    def _():
        for slot in range(slots):
            tiles = staged[slot].reshape(devices, tile_rows, LANES)
            out_ref[:, base + slot] = tiles.astype(jnp.bfloat16)


def chosen_packed(blocks, halo, kept, kept_count, devices):
    diag, lower, upper, sigma = blocks
    low, high = halo
    _, energies, cells, size, _ = diag.shape
    slots = kept.shape[1]
    order = packing_order(cells)
    tile_rows = energies * 2 * (PAIRS // devices)
    packed = (devices, cells * slots, tile_rows, LANES)
    block = (2, 1, 1, size, size)
    whole = pl.BlockSpec(packed, lambda i, e, *_: (0, 0, 0, 0))
    scratch = [
        pltpu.VMEM((3, 2, size, size), jnp.bfloat16),
        pltpu.VMEM((slots, LANES, LANES), jnp.float32),
        pltpu.VMEM((slots, devices * tile_rows, LANES), jnp.float32),
    ]

    def call(first, places, in_specs, extra, args):
        return pl.pallas_call(
            partial(lesser_kernel, order, first, devices),
            grid_spec=pltpu.PrefetchScalarGridSpec(
                num_scalar_prefetch=2,
                grid=(places, energies),
                in_specs=in_specs,
                out_specs=whole,
                scratch_shapes=scratch + extra,
            ),
            out_shape=jax.ShapeDtypeStruct(packed, jnp.bfloat16),
            compiler_params=pltpu.CompilerParams(vmem_limit_bytes=48 << 20),
            cost_estimate=pl.CostEstimate(
                flops=places * energies * 48 * size**3, bytes_accessed=places * energies * 6 * size * size * 4, transcendentals=0
            ),
        )(kept, kept_count, *args)

    def at(cell_of):
        return pl.BlockSpec(block, lambda i, e, *_: (0, e, cell_of(i), 0, 0))

    inside = at(lambda i: i + 1)
    first_part = call(
        True,
        cells - 2,
        [inside, inside, inside, inside, at(lambda i: i), at(lambda i: i + 2)],
        [],
        (diag, lower, upper, sigma, sigma, sigma),
    )
    outside = at(lambda i: i * (cells - 1))
    near = at(lambda i: 1 + i * (cells - 3))
    only = at(lambda i: 0)
    return call(
        False,
        2,
        [outside, outside, outside, outside, near, only, only, whole],
        [pltpu.VMEM((2, 2, size, size), jnp.bfloat16)],
        (diag, lower, upper, sigma, sigma, low, high, first_part),
    )


def mixing_kernel(cells, share, screened_ref, weight_ref, table):
    doubled = screened_ref.shape[1] // 2
    total = doubled // 2
    lane_count = table.shape[2]
    shape = (2 * doubled, lane_count)
    source = lax.broadcasted_iota(jnp.int32, shape, 0)
    lane = lax.broadcasted_iota(jnp.int32, shape, 1)
    offset = 2 * total - 2 - lane // (2 * share)
    part = (lane // share) % 2
    spot = lane % share
    for row in range(2 * share):
        own_part, own_spot = row // share, row % share
        wanted = jnp.where(part == own_part, 0, doubled) + offset
        sign = jnp.where(part > own_part, -1.0, 1.0)
        pick = jnp.where((source == wanted) & (spot == own_spot) & (offset >= 0), sign, 0.0)
        table[:, row, :] = jnp.dot(
            screened_ref[...], pick.astype(jnp.bfloat16), preferred_element_type=jnp.float32
        )
    size = weight_ref.shape[1]
    rows = 2 * share
    for cell in range(cells):
        for energy in range(total):
            start = (total - 1 - energy) * rows
            weight_ref[cell, energy * rows : (energy + 1) * rows, :] = table[
                cell, :, start : start + size
            ].astype(jnp.bfloat16)


def mixing_matrix(screened, devices):
    _, cells, doubled = screened.shape
    share = PAIRS // devices
    size = doubled * share
    return pl.pallas_call(
        partial(mixing_kernel, cells, share),
        out_shape=jax.ShapeDtypeStruct((cells, size, size), jnp.bfloat16),
        scratch_shapes=[pltpu.VMEM((cells, 2 * share, 2 * size), jnp.float32)],
        compiler_params=pltpu.CompilerParams(vmem_limit_bytes=48 << 20),
        cost_estimate=pl.CostEstimate(flops=1 << 20, bytes_accessed=1 << 20, transcendentals=0),
    )(jnp.concatenate([screened[0], screened[1]], axis=1))


def mix_kernel(order, group, count_ref, weight_ref, x_ref, y_ref):
    devices, _, tile_rows, _ = x_ref.shape
    ends = []
    end = jnp.int32(0)
    for cell in order[:-1]:
        end = end + count_ref[cell]
        ends.append(end)
    for slot in range(group):
        number = pl.program_id(0) * group + slot
        place = jnp.int32(0)
        for end in ends:
            place = place + jnp.where(number >= end, 1, 0)
        cell = jnp.int32(order[-1])
        for index, name in enumerate(order[:-1]):
            cell = jnp.where(place == index, name, cell)
        entries = x_ref[:, slot].reshape(devices * tile_rows, LANES)
        mixed = jnp.dot(weight_ref[cell], entries, preferred_element_type=jnp.float32)
        y_ref[:, slot] = mixed.astype(jnp.bfloat16).reshape(devices, tile_rows, LANES)


def mix(packed, weights, kept_count):
    devices, total, tile_rows, _ = packed.shape
    group = min(8, total)
    block = pl.BlockSpec((devices, group, tile_rows, LANES), lambda i, *_: (0, i, 0, 0))
    return pl.pallas_call(
        partial(mix_kernel, packing_order(kept_count.shape[0]), group),
        grid_spec=pltpu.PrefetchScalarGridSpec(
            num_scalar_prefetch=1,
            grid=(total // group,),
            in_specs=[pl.BlockSpec(weights.shape, lambda i, *_: (0, 0, 0)), block],
            out_specs=block,
        ),
        out_shape=jax.ShapeDtypeStruct(packed.shape, jnp.bfloat16),
        compiler_params=pltpu.CompilerParams(vmem_limit_bytes=48 << 20),
    )(kept_count, weights, packed)


def unpack_kernel(order, count_ref, y_ref, out_ref, rows):
    devices, total, tile_rows, _ = y_ref.shape
    _, energies, _, slots, _ = out_ref.shape
    cell = pl.program_id(0)
    position = jnp.int32(0)
    for index, name in enumerate(order):
        position = jnp.where(cell == name, index, position)
    base = slot_base(count_ref, order, position)
    for slot in range(slots):
        number = jnp.minimum(base + slot, total - 1)
        rows[:, pl.ds(slot * tile_rows, tile_rows), :] = y_ref[:, number].astype(jnp.float32)
    live = lax.broadcasted_iota(jnp.int32, (slots, LANES), 0) < count_ref[cell]
    share = PAIRS // devices
    for part in range(2):
        for energy in range(energies):
            for index in range(PAIRS):
                row = (energy * 2 + part) * share + index // devices
                entries = rows[index % devices, pl.ds(row, slots, stride=tile_rows), :]
                out_ref[part, energy, 0, :, index * LANES : (index + 1) * LANES] = jnp.where(
                    live, entries, 0.0
                ).astype(jnp.bfloat16)


def unpack(packed, kept_count, energies, slots):
    devices, total, tile_rows, _ = packed.shape
    cells = kept_count.shape[0]
    shape = (2, energies, cells, slots, SUB * SUB)
    return pl.pallas_call(
        partial(unpack_kernel, packing_order(cells)),
        grid_spec=pltpu.PrefetchScalarGridSpec(
            num_scalar_prefetch=1,
            grid=(cells,),
            in_specs=[pl.BlockSpec(packed.shape, lambda i, *_: (0, 0, 0, 0))],
            out_specs=pl.BlockSpec(
                (2, energies, 1, slots, SUB * SUB), lambda i, *_: (0, 0, i, 0, 0)
            ),
            scratch_shapes=[pltpu.VMEM((devices, slots * tile_rows, LANES), jnp.float32)],
        ),
        out_shape=jax.ShapeDtypeStruct(shape, jnp.bfloat16),
        compiler_params=pltpu.CompilerParams(vmem_limit_bytes=48 << 20),
    )(kept_count, packed)


def per_device(diag, lower, upper, sigma, screened, kept, kept_count):
    count = lax.axis_size("cell")
    devices = lax.axis_size("energy")
    forward = [(i, i + 1) for i in range(count - 1)]
    backward = [(target, source) for source, target in forward]
    low = lax.ppermute(sigma[:, :, -1:], "cell", forward)
    high = lax.ppermute(sigma[:, :, :1], "cell", backward)
    packed = chosen_packed((diag, lower, upper, sigma), (low, high), kept, kept_count, devices)
    weights = mixing_matrix(screened, devices)
    exchange = partial(lax.all_to_all, axis_name="energy", split_axis=0, concat_axis=0, tiled=True)
    mixed = mix(exchange(packed), weights, kept_count)
    return unpack(exchange(mixed), kept_count, sigma.shape[1], kept.shape[1])


def solution(mesh):
    placed = (
        P(None, "energy", "cell", None, None),
        P(None, "energy", "cell", None, None),
        P(None, "energy", "cell", None, None),
        P(None, "energy", "cell", None, None),
        P(None, "cell", None),
        P("cell", None),
        P("cell"),
    )
    return jax.shard_map(
        per_device,
        mesh=mesh,
        in_specs=placed,
        out_specs=P(None, "energy", "cell", None, None),
        check_vma=False,
    )
```

```python
from functools import partial

import jax
import jax.numpy as jnp
from jax import lax
from jax.experimental import pallas as pl
from jax.experimental.pallas import tpu as pltpu
from jax.sharding import PartitionSpec as P

SUB = 64
LANES = 2 * SUB
PAIRS = SUB // 2
STEP = 8


def packing_order(cell_count):
    interior = list(range(1, cell_count - 1))
    return interior + [0, cell_count - 1] if cell_count > 1 else [0]


def slot_base(count_ref, order, position):
    base = jnp.int32(0)
    for place, cell in enumerate(order[:-1]):
        base = base + jnp.where(place < position, count_ref[cell], 0)
    return base


def inner_products(factor, middle_r, middle_i):
    row = jnp.concatenate([factor[0], factor[1]], axis=1)
    real_part = jnp.dot(
        row, jnp.concatenate([middle_r, -middle_i], axis=0), preferred_element_type=jnp.float32
    )
    imag_part = jnp.dot(
        row, jnp.concatenate([middle_i, middle_r], axis=0), preferred_element_type=jnp.float32
    )
    return by_strips(real_part.astype(jnp.bfloat16), imag_part.astype(jnp.bfloat16))


def by_strips(real_part, imag_part):
    pieces = []
    for start in range(0, real_part.shape[0], SUB):
        pieces += [real_part[start : start + SUB], imag_part[start : start + SUB]]
    return jnp.concatenate(pieces, axis=0)


def paired_rows(product_ref, number, group):
    def rows(half, odd):
        start = half * SUB + group * 2 * STEP + odd
        return product_ref[number, pl.ds(start, STEP, stride=2), :]

    left = lax.broadcasted_iota(jnp.int32, (STEP, LANES), 1) < SUB
    top_even, top_odd = rows(0, 0), rows(0, 1)
    low_even, low_odd = rows(1, 0), rows(1, 1)
    real_part = jnp.where(left, top_even, low_odd) + pltpu.roll(
        jnp.where(left, top_odd, low_even), SUB, 1
    )
    imag_part = jnp.where(left, low_even, -top_odd) + pltpu.roll(
        jnp.where(left, low_odd, -top_even), SUB, 1
    )
    return real_part, imag_part


def sandwiches(factors, middles):
    inner = jnp.concatenate(
        [inner_products(factor, *middle) for factor, middle in zip(factors, middles)], axis=1
    )
    return lax.dot_general(
        inner,
        jnp.concatenate([by_strips(*factor) for factor in factors], axis=1),
        (((1,), (1,)), ((), ())),
        preferred_element_type=jnp.float32,
    )


def stage_slots(products, kept_ref, cell, energy, devices, tile_rows, product, staged):
    per_side = products.shape[0] // LANES
    share = PAIRS // devices
    for top in range(per_side):
        for side in range(per_side):
            product[top * per_side + side] = products[
                top * LANES : (top + 1) * LANES, side * LANES : (side + 1) * LANES
            ]
    for slot in range(kept_ref.shape[1]):
        number = kept_ref[cell, slot]
        for group in range(PAIRS // STEP):
            pair = paired_rows(product, number, group)
            device = (group * STEP) % devices
            for part in range(2):
                row = (energy * 2 + part) * share + group * STEP // devices
                start = device * tile_rows + row
                staged[slot, pl.ds(start, STEP, stride=tile_rows), :] = pair[part]


def slot_tiles(staged, slot, out_ref):
    devices, _, tile_rows, _ = out_ref.shape
    return staged[slot].reshape(devices, tile_rows, LANES).astype(jnp.bfloat16)


def local_kernel(order, devices, sizes, kept_ref, count_ref, screened_ref, *refs):
    sources, sigma_source = refs[:3], refs[3]
    out_ref, partial_ref, outer_ref, weight_ref, index_ref = refs[4:9]
    held, near, sigma, table, product, staged, held_sem, near_sem, outer_sem, sigma_sem = refs[9:]
    _, energies, cell_count, _, _ = sigma_source.shape
    slots = kept_ref.shape[1]
    places = cell_count - 2
    last = cell_count - 1
    diag, lower, upper = sources

    def moved(source, energy, cell, target, spot, sem):
        return pltpu.make_async_copy(
            source.at[:, energy, cell], target.at[:, energy, spot], sem
        )

    def sigma_copy(energy, cell):
        return moved(sigma_source, energy, cell, sigma, cell, sigma_sem.at[energy, cell])

    steps = []
    for position in range(places):
        for energy in range(energies):
            cells = [order[position] + 1] if position else [0, 1, 2]
            copies = [sigma_copy(energy, cell) for cell in cells]
            for term, source in enumerate(sources):
                copies.append(
                    moved(
                        source, energy, order[position], held.at[term], position,
                        held_sem.at[term, energy, position],
                    )
                )
            steps.append(copies)
    for edge, cell in enumerate((0, last)):
        for energy in range(energies):
            steps.append(
                [
                    moved(source, energy, cell, near.at[term], edge, near_sem.at[term, energy, edge])
                    for term, source in enumerate((diag, (upper, lower)[edge]))
                ]
            )
    outer_copies = [
        moved((lower, upper)[edge], energy, cell, outer_ref, edge, outer_sem.at[energy, edge])
        for edge, cell in enumerate((0, last))
        for energy in range(energies)
    ]
    ahead = 3
    for copies in steps[:ahead]:
        for copy in copies:
            copy.start()

    def arrive(step):
        if step + ahead < len(steps):
            for copy in steps[step + ahead]:
                copy.start()
        elif step + ahead == len(steps):
            for copy in outer_copies:
                copy.start()
        for copy in steps[step]:
            copy.wait()

    def pair_of(ref, energy, spot):
        return ref[0, energy, spot], ref[1, energy, spot]

    live = jnp.int32(0)
    for cell in range(cell_count):
        live = live + count_ref[cell]
    index = jnp.int32(0)
    for size in sizes[:-1]:
        index = index + jnp.where(live > size, 1, 0)
    index_ref[0] = index
    fill_mixing(screened_ref, weight_ref, table)

    step = 0
    for position in range(places):
        cell = order[position]
        base = slot_base(count_ref, order, position)
        for energy in range(energies):
            arrive(step)
            step += 1
            products = sandwiches(
                [pair_of(held.at[term], energy, position) for term in range(3)],
                [pair_of(sigma, energy, other) for other in (cell, cell - 1, cell + 1)],
            )
            stage_slots(
                products, kept_ref, cell, energy, devices, out_ref.shape[2],
                product.at[energy], staged,
            )
        for slot in range(slots):
            out_ref[:, base + slot] = slot_tiles(staged, slot, out_ref)
    for edge, cell in enumerate((0, last)):
        for energy in range(energies):
            arrive(step)
            step += 1
            partial_ref[edge, energy] = sandwiches(
                [pair_of(near.at[term], energy, edge) for term in range(2)],
                [pair_of(sigma, energy, other) for other in (cell, (1, last - 1)[edge])],
            )
    for copy in outer_copies:
        copy.wait()


def edge_kernel(order, kept_ref, count_ref, partial_ref, outer_ref, low, high, earlier, *refs):
    out_ref, product, staged = refs
    _, energies, edge_count, _, _ = outer_ref.shape
    devices, total, tile_rows, _ = out_ref.shape
    ready = min(earlier.shape[1], total)
    out_ref[:, :ready] = earlier[:, :ready]
    for edge, halo in enumerate((low, high)):
        position = len(order) - edge_count + edge
        cell = order[position]
        base = slot_base(count_ref, order, position)
        for energy in range(energies):
            products = partial_ref[edge, energy] + sandwiches(
                [(outer_ref[0, energy, edge], outer_ref[1, energy, edge])],
                [(halo[0, energy, 0], halo[1, energy, 0])],
            )
            stage_slots(
                products, kept_ref, cell, energy, devices, tile_rows, product.at[energy], staged
            )
        for slot in range(kept_ref.shape[1]):

            @pl.when(slot < count_ref[cell])
            def _(slot=slot, base=base):
                out_ref[:, base + slot] = slot_tiles(staged, slot, out_ref)


SCALARS = pl.BlockSpec(memory_space=pltpu.SMEM)
VECTORS = pl.BlockSpec(memory_space=pltpu.VMEM)
STAYING = pl.BlockSpec(memory_space=pltpu.HBM)


def cost_of(places, energies, size):
    return pl.CostEstimate(
        flops=places * energies * 48 * size**3,
        bytes_accessed=places * energies * 6 * size * size * 4,
        transcendentals=0,
    )


def fill_scratch(energies, size, slots, rows):
    return [
        pltpu.VMEM((energies, (size // SUB) ** 2, LANES, LANES), jnp.float32),
        pltpu.VMEM((slots, rows, LANES), jnp.float32),
    ]


def local_part(blocks, screened, kept, kept_count, devices, sizes):
    _, energies, cells, size, _ = blocks[0].shape
    slots = kept.shape[1]
    share = PAIRS // devices
    tile_rows = energies * 2 * share
    rows = 2 * screened.shape[2] // 2 * share
    places = cells - 2
    wide = 2 * size

    def bfloat(*shape):
        return jax.ShapeDtypeStruct(shape, jnp.bfloat16)

    return pl.pallas_call(
        partial(local_kernel, packing_order(cells), devices, sizes),
        in_specs=[SCALARS, SCALARS, VECTORS] + [STAYING] * 4,
        out_specs=[VECTORS] * 4 + [SCALARS],
        out_shape=[
            bfloat(devices, places * slots, tile_rows, LANES),
            jax.ShapeDtypeStruct((2, energies, wide, wide), jnp.float32),
            bfloat(2, energies, 2, size, size),
            bfloat(cells, rows, rows),
            jax.ShapeDtypeStruct((1,), jnp.int32),
        ],
        scratch_shapes=[
            pltpu.VMEM((3, 2, energies, places, size, size), jnp.bfloat16),
            pltpu.VMEM((2, 2, energies, 2, size, size), jnp.bfloat16),
            pltpu.VMEM((2, energies, cells, size, size), jnp.bfloat16),
            pltpu.VMEM((cells, 2 * share, 2 * rows), jnp.float32),
        ]
        + fill_scratch(energies, size, slots, devices * tile_rows)
        + [
            pltpu.SemaphoreType.DMA((3, energies, places)),
            pltpu.SemaphoreType.DMA((2, energies, 2)),
            pltpu.SemaphoreType.DMA((energies, 2)),
            pltpu.SemaphoreType.DMA((energies, cells)),
        ],
        compiler_params=pltpu.CompilerParams(vmem_limit_bytes=55 << 20),
        cost_estimate=cost_of(cells, energies, size),
    )(kept, kept_count, screened, *blocks)


def edges(total, partial_sum, outer, halo, earlier, kept, kept_count):
    _, energies, _, size, _ = outer.shape
    devices, _, tile_rows, _ = earlier.shape
    return pl.pallas_call(
        partial(edge_kernel, packing_order(kept.shape[0])),
        in_specs=[SCALARS, SCALARS] + [VECTORS] * 5,
        out_specs=VECTORS,
        out_shape=jax.ShapeDtypeStruct((devices, total, tile_rows, LANES), jnp.bfloat16),
        scratch_shapes=fill_scratch(energies, size, kept.shape[1], devices * tile_rows),
        compiler_params=pltpu.CompilerParams(vmem_limit_bytes=32 << 20),
        cost_estimate=cost_of(1, energies, size),
    )(kept, kept_count, partial_sum, outer, *halo, earlier)


def border_kernel(sigma, first, last, sems):
    cells = sigma.shape[2]
    copies = [
        pltpu.make_async_copy(sigma.at[:, :, pl.ds(0, 1)], first, sems.at[0]),
        pltpu.make_async_copy(sigma.at[:, :, pl.ds(cells - 1, 1)], last, sems.at[1]),
    ]
    for copy in copies:
        copy.start()
    for copy in copies:
        copy.wait()


def border(sigma):
    shape = jax.ShapeDtypeStruct(sigma.shape[:2] + (1,) + sigma.shape[3:], sigma.dtype)
    return pl.pallas_call(
        border_kernel,
        in_specs=[STAYING],
        out_specs=[VECTORS] * 2,
        out_shape=[shape, shape],
        scratch_shapes=[pltpu.SemaphoreType.DMA((2,))],
        compiler_params=pltpu.CompilerParams(vmem_limit_bytes=60 << 20),
    )(sigma)


def fill_mixing(screened_ref, weight_ref, table):
    _, cells, doubled = screened_ref.shape
    _, rows, lane_count = table.shape
    total, share = doubled // 2, rows // 2
    shape = (2 * doubled, lane_count)
    source = lax.broadcasted_iota(jnp.int32, shape, 0)
    lane = lax.broadcasted_iota(jnp.int32, shape, 1)
    offset = 2 * total - 2 - lane // rows
    part = (lane // share) % 2
    spot = lane % share
    both = jnp.concatenate([screened_ref[0], screened_ref[1]], axis=1)
    for row in range(rows):
        own_part, own_spot = row // share, row % share
        wanted = jnp.where(part == own_part, 0, doubled) + offset
        sign = jnp.where(part > own_part, -1.0, 1.0)
        pick = jnp.where((source == wanted) & (spot == own_spot) & (offset >= 0), sign, 0.0)
        table[:, row, :] = jnp.dot(
            both, pick.astype(jnp.bfloat16), preferred_element_type=jnp.float32
        )
    size = weight_ref.shape[1]
    for cell in range(cells):
        for energy in range(total):
            start = (total - 1 - energy) * rows
            weight_ref[cell, energy * rows : (energy + 1) * rows, :] = table[
                cell, :, start : start + size
            ].astype(jnp.bfloat16)


def mix_kernel(order, count_ref, weight_ref, x_ref, y_ref):
    devices, total, tile_rows, _ = x_ref.shape
    ends = []
    end = jnp.int32(0)
    for cell in order[:-1]:
        end = end + count_ref[cell]
        ends.append(end)
    for slot in range(total):
        cell = jnp.int32(order[-1])
        for name, end in reversed(list(zip(order, ends))):
            cell = jnp.where(slot < end, name, cell)
        entries = x_ref[:, slot].reshape(devices * tile_rows, LANES)
        mixed = jnp.dot(weight_ref[cell], entries, preferred_element_type=jnp.float32)
        y_ref[:, slot] = mixed.astype(jnp.bfloat16).reshape(devices, tile_rows, LANES)


def mix(packed, weights, kept_count):
    return pl.pallas_call(
        partial(mix_kernel, packing_order(kept_count.shape[0])),
        in_specs=[SCALARS, VECTORS, VECTORS],
        out_specs=VECTORS,
        out_shape=jax.ShapeDtypeStruct(packed.shape, jnp.bfloat16),
        compiler_params=pltpu.CompilerParams(vmem_limit_bytes=16 << 20),
    )(kept_count, weights, packed)


def unpack_kernel(order, count_ref, y_ref, out_ref, rows, cells_out, sems):
    devices, total, tile_rows, _ = y_ref.shape
    _, energies, cell_count, slots, _ = out_ref.shape
    share = PAIRS // devices
    copies = []
    for position, cell in enumerate(order):
        base = slot_base(count_ref, order, position)
        held = rows.at[position % 2]
        for slot in range(slots):
            number = jnp.minimum(base + slot, total - 1)
            held[:, slot * tile_rows : (slot + 1) * tile_rows, :] = y_ref[:, number].astype(
                jnp.float32
            )
        live = lax.broadcasted_iota(jnp.int32, (slots, LANES), 0) < count_ref[cell]
        for part in range(2):
            for energy in range(energies):
                for index in range(PAIRS):
                    row = (energy * 2 + part) * share + index // devices
                    entries = held[index % devices, pl.ds(row, slots, stride=tile_rows), :]
                    cells_out[part, energy, cell, :, index * LANES : (index + 1) * LANES] = (
                        jnp.where(live, entries, 0.0).astype(jnp.bfloat16)
                    )
        copy = pltpu.make_async_copy(cells_out.at[:, :, cell], out_ref.at[:, :, cell], sems.at[cell])
        copy.start()
        copies.append(copy)
    for copy in copies:
        copy.wait()


def unpack(packed, kept_count, energies, slots):
    devices, total, tile_rows, _ = packed.shape
    cells = kept_count.shape[0]
    shape = (2, energies, cells, slots, SUB * SUB)
    return pl.pallas_call(
        partial(unpack_kernel, packing_order(cells)),
        in_specs=[SCALARS, VECTORS],
        out_specs=STAYING,
        out_shape=pltpu.HBM(shape, jnp.bfloat16),
        scratch_shapes=[
            pltpu.VMEM((2, devices, slots * tile_rows, LANES), jnp.float32),
            pltpu.VMEM(shape, jnp.bfloat16),
            pltpu.SemaphoreType.DMA((cells,)),
        ],
        compiler_params=pltpu.CompilerParams(vmem_limit_bytes=16 << 20),
    )(kept_count, packed)


def per_device(diag, lower, upper, sigma, screened, kept, kept_count):
    count = lax.axis_size("cell")
    devices = lax.axis_size("energy")
    forward = [(i, i + 1) for i in range(count - 1)]
    backward = [(target, source) for source, target in forward]
    first, last = border(sigma)
    low = lax.ppermute(last, "cell", forward)
    high = lax.ppermute(first, "cell", backward)
    energies, slots = sigma.shape[1], kept.shape[1]
    full = kept.shape[0] * slots
    sizes = [full * eighths // 8 for eighths in (4, 5, 6, 7, 8)]
    earlier, partial_sum, outer, weights, index = local_part(
        (diag, lower, upper, sigma), screened, kept, kept_count, devices, sizes
    )
    exchange = partial(lax.all_to_all, axis_name="energy", split_axis=0, concat_axis=0, tiled=True)

    def with_slots(total, partial_sum, outer, halo, earlier, weights, kept, kept_count):
        packed = edges(total, partial_sum, outer, halo, earlier, kept, kept_count)
        mixed = mix(exchange(packed), weights, kept_count)
        return unpack(exchange(mixed), kept_count, energies, slots)

    return lax.switch(
        index[0],
        [partial(with_slots, size) for size in sizes],
        partial_sum, outer, (low, high), earlier, weights, kept, kept_count,
    )


def solution(mesh):
    placed = (
        P(None, "energy", "cell", None, None),
        P(None, "energy", "cell", None, None),
        P(None, "energy", "cell", None, None),
        P(None, "energy", "cell", None, None),
        P(None, "cell", None),
        P("cell", None),
        P("cell"),
    )
    return jax.shard_map(
        per_device,
        mesh=mesh,
        in_specs=placed,
        out_specs=P(None, "energy", "cell", None, None),
        check_vma=False,
    )
```

```python
from functools import partial

import jax
import jax.numpy as jnp
from jax import lax
from jax.experimental import pallas as pl
from jax.experimental.pallas import tpu as pltpu
from jax.sharding import PartitionSpec as P

SUB = 64
LANES = 2 * SUB
PAIRS = SUB // 2
STEP = 8
PITCH = 24


def pairwise(devices):
    return devices <= STEP and devices & (devices - 1) == 0


def partners(devices):
    if not pairwise(devices):
        return list(range(devices))
    others = sorted(
        range(1, devices), key=lambda bits: (-bin(bits >> 1).count("1"), bits & 1, bits)
    )
    return [0] + others


def partner_of(bits, devices):
    if not pairwise(devices):
        return bits
    return lax.axis_index("energy") ^ bits


def exchange(parts):
    devices = len(parts)
    if not pairwise(devices):
        sent = lax.all_to_all(jnp.stack(parts), "energy", split_axis=0, concat_axis=0, tiled=True)
        return [sent[index] for index in range(devices)]
    return [parts[0]] + [
        lax.ppermute(part, "energy", [(source, source ^ bits) for source in range(devices)])
        for bits, part in zip(partners(devices)[1:], parts[1:])
    ]


def packing_order(cell_count):
    interior = list(range(1, cell_count - 1))
    return interior + [0, cell_count - 1] if cell_count > 1 else [0]


def slot_base(count_ref, order, position):
    base = jnp.int32(0)
    for place, cell in enumerate(order[:-1]):
        base = base + jnp.where(place < position, count_ref[cell], 0)
    return base


def inner_products(factor, middle_r, middle_i):
    row = jnp.concatenate([factor[0], factor[1]], axis=1)
    real_part = jnp.dot(
        row, jnp.concatenate([middle_r, -middle_i], axis=0), preferred_element_type=jnp.float32
    )
    imag_part = jnp.dot(
        row, jnp.concatenate([middle_i, middle_r], axis=0), preferred_element_type=jnp.float32
    )
    return by_strips(real_part.astype(jnp.bfloat16), imag_part.astype(jnp.bfloat16))


def by_strips(real_part, imag_part):
    pieces = []
    for start in range(0, real_part.shape[0], SUB):
        pieces += [real_part[start : start + SUB], imag_part[start : start + SUB]]
    return jnp.concatenate(pieces, axis=0)


def paired_rows(product_ref, number, group):
    def rows(half, odd):
        start = half * SUB + group * 2 * STEP + odd
        return product_ref[number, pl.ds(start, STEP, stride=2), :]

    left = lax.broadcasted_iota(jnp.int32, (STEP, LANES), 1) < SUB
    top_even, top_odd = rows(0, 0), rows(0, 1)
    low_even, low_odd = rows(1, 0), rows(1, 1)
    real_part = jnp.where(left, top_even, low_odd) + pltpu.roll(
        jnp.where(left, top_odd, low_even), SUB, 1
    )
    imag_part = jnp.where(left, low_even, -top_odd) + pltpu.roll(
        jnp.where(left, low_odd, -top_even), SUB, 1
    )
    return real_part, imag_part


def sandwiches(factors, middles):
    inner = jnp.concatenate(
        [inner_products(factor, *middle) for factor, middle in zip(factors, middles)], axis=1
    )
    return lax.dot_general(
        inner,
        jnp.concatenate([by_strips(*factor) for factor in factors], axis=1),
        (((1,), (1,)), ((), ())),
        preferred_element_type=jnp.float32,
    )


def stage_slots(products, kept_ref, cell, energy, devices, tile_rows, product, staged):
    per_side = products.shape[0] // LANES
    share = PAIRS // devices
    for top in range(per_side):
        for side in range(per_side):
            product[top * per_side + side] = products[
                top * LANES : (top + 1) * LANES, side * LANES : (side + 1) * LANES
            ]
    for slot in range(kept_ref.shape[1]):
        number = kept_ref[cell, slot]
        for group in range(PAIRS // STEP):
            pair = paired_rows(product, number, group)
            device = (group * STEP) % devices
            for part in range(2):
                row = (energy * 2 + part) * share + group * STEP // devices
                start = device * tile_rows + row
                staged[slot, pl.ds(start, STEP, stride=tile_rows), :] = pair[part]


def slot_tiles(staged, slot, out_ref):
    devices, _, tile_rows, _ = out_ref.shape
    return staged[slot].reshape(devices, tile_rows, LANES).astype(jnp.bfloat16)


def local_kernel(order, devices, sizes, kept_ref, count_ref, screened_ref, *refs):
    sources, sigma_source = refs[:3], refs[3]
    out_ref, partial_ref, outer_ref, weight_ref, index_ref = refs[4:9]
    held, near, sigma, table, product, staged, held_sem, near_sem, outer_sem, sigma_sem = refs[9:]
    _, energies, cell_count, _, _ = sigma_source.shape
    slots = kept_ref.shape[1]
    places = cell_count - 2
    last = cell_count - 1
    diag, lower, upper = sources

    def moved(source, energy, cell, target, spot, sem):
        return pltpu.make_async_copy(
            source.at[:, energy, cell], target.at[:, energy, spot], sem
        )

    def sigma_copy(energy, cell):
        return moved(sigma_source, energy, cell, sigma, cell, sigma_sem.at[energy, cell])

    steps = []
    for position in range(places):
        for energy in range(energies):
            cells = [order[position] + 1] if position else [0, 1, 2]
            copies = [sigma_copy(energy, cell) for cell in cells]
            for term, source in enumerate(sources):
                copies.append(
                    moved(
                        source, energy, order[position], held.at[term], position,
                        held_sem.at[term, energy, position],
                    )
                )
            steps.append(copies)
    for edge, cell in enumerate((0, last)):
        for energy in range(energies):
            steps.append(
                [
                    moved(source, energy, cell, near.at[term], edge, near_sem.at[term, energy, edge])
                    for term, source in enumerate((diag, (upper, lower)[edge]))
                ]
            )
    outer_copies = [
        moved((lower, upper)[edge], energy, cell, outer_ref, edge, outer_sem.at[energy, edge])
        for edge, cell in enumerate((0, last))
        for energy in range(energies)
    ]
    ahead = 3
    for copies in steps[:ahead]:
        for copy in copies:
            copy.start()

    def arrive(step):
        if step + ahead < len(steps):
            for copy in steps[step + ahead]:
                copy.start()
        elif step + ahead == len(steps):
            for copy in outer_copies:
                copy.start()
        for copy in steps[step]:
            copy.wait()

    def pair_of(ref, energy, spot):
        return ref[0, energy, spot], ref[1, energy, spot]

    live = jnp.int32(0)
    for cell in range(cell_count):
        live = live + count_ref[cell]
    index = jnp.int32(0)
    for size in sizes[:-1]:
        index = index + jnp.where(live > size, 1, 0)
    index_ref[0] = index
    fill_mixing(screened_ref, weight_ref, table)

    step = 0
    for position in range(places):
        cell = order[position]
        base = slot_base(count_ref, order, position)
        for energy in range(energies):
            arrive(step)
            step += 1
            products = sandwiches(
                [pair_of(held.at[term], energy, position) for term in range(3)],
                [pair_of(sigma, energy, other) for other in (cell, cell - 1, cell + 1)],
            )
            stage_slots(
                products, kept_ref, cell, energy, devices, out_ref.shape[2],
                product.at[energy], staged,
            )
        for slot in range(slots):
            out_ref[:, base + slot] = slot_tiles(staged, slot, out_ref)
    for edge, cell in enumerate((0, last)):
        for energy in range(energies):
            arrive(step)
            step += 1
            partial_ref[edge, energy] = sandwiches(
                [pair_of(near.at[term], energy, edge) for term in range(2)],
                [pair_of(sigma, energy, other) for other in (cell, (1, last - 1)[edge])],
            )
    for copy in outer_copies:
        copy.wait()


def edge_kernel(order, kept_ref, count_ref, partial_ref, outer_ref, low, high, earlier, *refs):
    *outs, out_ref, product, staged = refs
    _, energies, edge_count, _, _ = outer_ref.shape
    devices, total, tile_rows, _ = out_ref.shape
    ready = min(earlier.shape[1], total)
    out_ref[:, :ready] = earlier[:, :ready]
    for edge, halo in enumerate((low, high)):
        position = len(order) - edge_count + edge
        cell = order[position]
        base = slot_base(count_ref, order, position)
        for energy in range(energies):
            products = partial_ref[edge, energy] + sandwiches(
                [(outer_ref[0, energy, edge], outer_ref[1, energy, edge])],
                [(halo[0, energy, 0], halo[1, energy, 0])],
            )
            stage_slots(
                products, kept_ref, cell, energy, devices, tile_rows, product.at[energy], staged
            )
        for slot in range(kept_ref.shape[1]):

            @pl.when(slot < count_ref[cell])
            def _(slot=slot, base=base):
                out_ref[:, base + slot] = slot_tiles(staged, slot, out_ref)

    for bits, out in zip(partners(devices), outs):
        out[...] = out_ref[partner_of(bits, devices)]


SCALARS = pl.BlockSpec(memory_space=pltpu.SMEM)
VECTORS = pl.BlockSpec(memory_space=pltpu.VMEM)
STAYING = pl.BlockSpec(memory_space=pltpu.HBM)


def cost_of(places, energies, size):
    return pl.CostEstimate(
        flops=places * energies * 48 * size**3,
        bytes_accessed=places * energies * 6 * size * size * 4,
        transcendentals=0,
    )


def fill_scratch(energies, size, slots, rows):
    return [
        pltpu.VMEM((energies, (size // SUB) ** 2, LANES, LANES), jnp.float32),
        pltpu.VMEM((slots, rows, LANES), jnp.float32),
    ]


def local_part(blocks, screened, kept, kept_count, devices, sizes):
    _, energies, cells, size, _ = blocks[0].shape
    slots = kept.shape[1]
    share = PAIRS // devices
    tile_rows = energies * 2 * share
    rows = 2 * screened.shape[2] // 2 * share
    places = cells - 2
    wide = 2 * size

    def bfloat(*shape):
        return jax.ShapeDtypeStruct(shape, jnp.bfloat16)

    return pl.pallas_call(
        partial(local_kernel, packing_order(cells), devices, sizes),
        in_specs=[SCALARS, SCALARS, VECTORS] + [STAYING] * 4,
        out_specs=[VECTORS] * 4 + [SCALARS],
        out_shape=[
            bfloat(devices, places * slots, tile_rows, LANES),
            jax.ShapeDtypeStruct((2, energies, wide, wide), jnp.float32),
            bfloat(2, energies, 2, size, size),
            bfloat(cells, rows, rows),
            jax.ShapeDtypeStruct((1,), jnp.int32),
        ],
        scratch_shapes=[
            pltpu.VMEM((3, 2, energies, places, size, size), jnp.bfloat16),
            pltpu.VMEM((2, 2, energies, 2, size, size), jnp.bfloat16),
            pltpu.VMEM((2, energies, cells, size, size), jnp.bfloat16),
            pltpu.VMEM((cells, 2 * share, 2 * rows), jnp.float32),
        ]
        + fill_scratch(energies, size, slots, devices * tile_rows)
        + [
            pltpu.SemaphoreType.DMA((3, energies, places)),
            pltpu.SemaphoreType.DMA((2, energies, 2)),
            pltpu.SemaphoreType.DMA((energies, 2)),
            pltpu.SemaphoreType.DMA((energies, cells)),
        ],
        compiler_params=pltpu.CompilerParams(vmem_limit_bytes=55 << 20),
        cost_estimate=cost_of(cells, energies, size),
    )(kept, kept_count, screened, *blocks)


def edges(total, partial_sum, outer, halo, earlier, kept, kept_count):
    _, energies, _, size, _ = outer.shape
    devices, _, tile_rows, _ = earlier.shape
    return pl.pallas_call(
        partial(edge_kernel, packing_order(kept.shape[0])),
        in_specs=[SCALARS, SCALARS] + [VECTORS] * 5,
        out_specs=[VECTORS] * devices,
        out_shape=[jax.ShapeDtypeStruct((total, tile_rows, LANES), jnp.bfloat16)] * devices,
        scratch_shapes=[pltpu.VMEM((devices, total, tile_rows, LANES), jnp.bfloat16)]
        + fill_scratch(energies, size, kept.shape[1], devices * tile_rows),
        compiler_params=pltpu.CompilerParams(vmem_limit_bytes=32 << 20),
        cost_estimate=cost_of(1, energies, size),
    )(kept, kept_count, partial_sum, outer, *halo, earlier)


def fill_mixing(screened_ref, weight_ref, table):
    _, cells, doubled = screened_ref.shape
    _, rows, lane_count = table.shape
    total, share = doubled // 2, rows // 2
    shape = (2 * doubled, lane_count)
    source = lax.broadcasted_iota(jnp.int32, shape, 0)
    lane = lax.broadcasted_iota(jnp.int32, shape, 1)
    offset = 2 * total - 2 - lane // rows
    part = (lane // share) % 2
    spot = lane % share
    both = jnp.concatenate([screened_ref[0], screened_ref[1]], axis=1)
    for row in range(rows):
        own_part, own_spot = row // share, row % share
        wanted = jnp.where(part == own_part, 0, doubled) + offset
        sign = jnp.where(part > own_part, -1.0, 1.0)
        pick = jnp.where((source == wanted) & (spot == own_spot) & (offset >= 0), sign, 0.0)
        table[:, row, :] = jnp.dot(
            both, pick.astype(jnp.bfloat16), preferred_element_type=jnp.float32
        )
    size = weight_ref.shape[1]
    for cell in range(cells):
        for energy in range(total):
            start = (total - 1 - energy) * rows
            weight_ref[cell, energy * rows : (energy + 1) * rows, :] = table[
                cell, :, start : start + size
            ].astype(jnp.bfloat16)


def mix_kernel(order, count_ref, weight_ref, *refs):
    parts, outs, x_ref, y_ref = refs[: len(refs) // 2 - 1], refs[len(refs) // 2 - 1 : -2], *refs[-2:]
    devices, total, tile_rows, _ = x_ref.shape
    for bits, part in zip(partners(devices), parts):
        x_ref[partner_of(bits, devices)] = part[...]
    ends = []
    end = jnp.int32(0)
    for cell in order[:-1]:
        end = end + count_ref[cell]
        ends.append(end)
    for slot in range(total):
        cell = jnp.int32(order[-1])
        for name, end in reversed(list(zip(order, ends))):
            cell = jnp.where(slot < end, name, cell)
        entries = x_ref[:, slot].reshape(devices * tile_rows, LANES)
        mixed = jnp.dot(weight_ref[cell], entries, preferred_element_type=jnp.float32)
        y_ref[:, slot] = mixed.astype(jnp.bfloat16).reshape(devices, tile_rows, LANES)
    for bits, out in zip(partners(devices), outs):
        out[...] = y_ref[partner_of(bits, devices)]


def mix(parts, weights, kept_count):
    devices = len(parts)
    return pl.pallas_call(
        partial(mix_kernel, packing_order(kept_count.shape[0])),
        in_specs=[SCALARS, VECTORS] + [VECTORS] * devices,
        out_specs=[VECTORS] * devices,
        out_shape=[jax.ShapeDtypeStruct(parts[0].shape, jnp.bfloat16)] * devices,
        scratch_shapes=[pltpu.VMEM((devices, *parts[0].shape), jnp.bfloat16)] * 2,
        compiler_params=pltpu.CompilerParams(vmem_limit_bytes=16 << 20),
    )(kept_count, weights, *parts)


def unpack_kernel(order, count_ref, *refs):
    *parts, out_ref, rows, cells_out, sems = refs
    devices = len(parts)
    total, tile_rows, _ = parts[0].shape
    _, energies, cell_count, slots, _ = out_ref.shape
    share = PAIRS // devices
    copies = []
    for position, cell in enumerate(order):
        base = slot_base(count_ref, order, position)
        held = rows.at[position % 2]
        for slot in range(slots):
            number = jnp.minimum(base + slot, total - 1)
            start = slot * PITCH
            for bits, part in zip(partners(devices), parts):
                held[partner_of(bits, devices), start : start + tile_rows, :] = part[
                    number
                ].astype(jnp.float32)
        live = lax.broadcasted_iota(jnp.int32, (slots, LANES), 0) < count_ref[cell]
        for part in range(2):
            for energy in range(energies):
                for index in range(PAIRS):
                    row = (energy * 2 + part) * share + index // devices
                    entries = held[index % devices, pl.ds(row, slots, stride=PITCH), :]
                    cells_out[part, energy, cell, :, index * LANES : (index + 1) * LANES] = (
                        jnp.where(live, entries, 0.0).astype(jnp.bfloat16)
                    )
        copy = pltpu.make_async_copy(cells_out.at[:, :, cell], out_ref.at[:, :, cell], sems.at[cell])
        copy.start()
        copies.append(copy)
    for copy in copies:
        copy.wait()


def unpack(parts, kept_count, energies, slots):
    devices = len(parts)
    cells = kept_count.shape[0]
    shape = (2, energies, cells, slots, SUB * SUB)
    return pl.pallas_call(
        partial(unpack_kernel, packing_order(cells)),
        in_specs=[SCALARS] + [VECTORS] * devices,
        out_specs=STAYING,
        out_shape=pltpu.HBM(shape, jnp.bfloat16),
        scratch_shapes=[
            pltpu.VMEM((2, devices, slots * PITCH, LANES), jnp.float32),
            pltpu.VMEM(shape, jnp.bfloat16),
            pltpu.SemaphoreType.DMA((cells,)),
        ],
        compiler_params=pltpu.CompilerParams(vmem_limit_bytes=16 << 20),
    )(kept_count, *parts)


def per_device(diag, lower, upper, sigma, screened, kept, kept_count):
    count = lax.axis_size("cell")
    devices = lax.axis_size("energy")
    forward = [(i, i + 1) for i in range(count - 1)]
    backward = [(target, source) for source, target in forward]
    low = lax.ppermute(sigma[:, :, -1:], "cell", forward)
    high = lax.ppermute(sigma[:, :, :1], "cell", backward)
    energies, slots = sigma.shape[1], kept.shape[1]
    full = kept.shape[0] * slots
    sizes = [full * eighths // 8 for eighths in (4, 5, 6, 7, 8)]
    earlier, partial_sum, outer, weights, index = local_part(
        (diag, lower, upper, sigma), screened, kept, kept_count, devices, sizes
    )

    def with_slots(total, partial_sum, outer, halo, earlier, weights, kept, kept_count):
        parts = edges(total, partial_sum, outer, halo, earlier, kept, kept_count)
        mixed = mix(exchange(parts), weights, kept_count)
        return unpack(exchange(mixed), kept_count, energies, slots)

    return lax.switch(
        index[0],
        [partial(with_slots, size) for size in sizes],
        partial_sum, outer, (low, high), earlier, weights, kept, kept_count,
    )


def solution(mesh):
    placed = (
        P(None, "energy", "cell", None, None),
        P(None, "energy", "cell", None, None),
        P(None, "energy", "cell", None, None),
        P(None, "energy", "cell", None, None),
        P(None, "cell", None),
        P("cell", None),
        P("cell"),
    )
    return jax.shard_map(
        per_device,
        mesh=mesh,
        in_specs=placed,
        out_specs=P(None, "energy", "cell", None, None),
        check_vma=False,
    )
```

```python
from functools import partial

import jax
import jax.numpy as jnp
from jax import lax
from jax.experimental import pallas as pl
from jax.experimental.pallas import tpu as pltpu
from jax.sharding import PartitionSpec as P

SUB = 64
LANES = 2 * SUB
PAIRS = SUB // 2
STEP = 8


def pairwise(devices):
    return devices <= STEP and devices & (devices - 1) == 0


def partners(devices):
    if not pairwise(devices):
        return list(range(devices))
    others = sorted(
        range(1, devices), key=lambda bits: (-bin(bits >> 1).count("1"), bits & 1, bits)
    )
    return [0] + others


def partner_of(bits, devices):
    if not pairwise(devices):
        return bits
    return lax.axis_index("energy") ^ bits


def exchange(parts):
    devices = len(parts)
    if not pairwise(devices):
        sent = lax.all_to_all(jnp.stack(parts), "energy", split_axis=0, concat_axis=0, tiled=True)
        return [sent[index] for index in range(devices)]
    return [parts[0]] + [
        lax.ppermute(part, "energy", [(source, source ^ bits) for source in range(devices)])
        for bits, part in zip(partners(devices)[1:], parts[1:])
    ]


def packing_order(cell_count):
    interior = list(range(1, cell_count - 1))
    return interior + [0, cell_count - 1] if cell_count > 1 else [0]


def slot_base(count_ref, order, position):
    base = jnp.int32(0)
    for place, cell in enumerate(order[:-1]):
        base = base + jnp.where(place < position, count_ref[cell], 0)
    return base


def inner_products(factor, middle_r, middle_i):
    row = jnp.concatenate([factor[0], factor[1]], axis=1)
    real_part = jnp.dot(
        row, jnp.concatenate([middle_r, -middle_i], axis=0), preferred_element_type=jnp.float32
    )
    imag_part = jnp.dot(
        row, jnp.concatenate([middle_i, middle_r], axis=0), preferred_element_type=jnp.float32
    )
    return by_strips(real_part.astype(jnp.bfloat16), imag_part.astype(jnp.bfloat16))


def by_strips(real_part, imag_part):
    pieces = []
    for start in range(0, real_part.shape[0], SUB):
        pieces += [real_part[start : start + SUB], imag_part[start : start + SUB]]
    return jnp.concatenate(pieces, axis=0)


def paired_rows(product_ref, number, group):
    def rows(half, odd):
        start = half * SUB + group * 2 * STEP + odd
        return product_ref[number, pl.ds(start, STEP, stride=2), :]

    left = lax.broadcasted_iota(jnp.int32, (STEP, LANES), 1) < SUB
    top_even, top_odd = rows(0, 0), rows(0, 1)
    low_even, low_odd = rows(1, 0), rows(1, 1)
    real_part = jnp.where(left, top_even, low_odd) + pltpu.roll(
        jnp.where(left, top_odd, low_even), SUB, 1
    )
    imag_part = jnp.where(left, low_even, -top_odd) + pltpu.roll(
        jnp.where(left, low_odd, -top_even), SUB, 1
    )
    return real_part, imag_part


def sandwiches(factors, middles):
    inner = jnp.concatenate(
        [inner_products(factor, *middle) for factor, middle in zip(factors, middles)], axis=1
    )
    return lax.dot_general(
        inner,
        jnp.concatenate([by_strips(*factor) for factor in factors], axis=1),
        (((1,), (1,)), ((), ())),
        preferred_element_type=jnp.float32,
    )


def stage_slots(products, kept_ref, cell, energy, devices, tile_rows, product, staged):
    per_side = products.shape[0] // LANES
    share = PAIRS // devices
    for top in range(per_side):
        for side in range(per_side):
            product[top * per_side + side] = products[
                top * LANES : (top + 1) * LANES, side * LANES : (side + 1) * LANES
            ]
    for slot in range(kept_ref.shape[1]):
        number = kept_ref[cell, slot]
        for group in range(PAIRS // STEP):
            pair = paired_rows(product, number, group)
            device = (group * STEP) % devices
            for part in range(2):
                row = (energy * 2 + part) * share + group * STEP // devices
                start = device * tile_rows + row
                staged[slot, pl.ds(start, STEP, stride=tile_rows), :] = pair[part]


def slot_tiles(staged, slot, out_ref):
    devices, _, tile_rows, _ = out_ref.shape
    return staged[slot].reshape(devices, tile_rows, LANES).astype(jnp.bfloat16)


def local_kernel(order, devices, sizes, kept_ref, count_ref, screened_ref, *refs):
    sources, sigma_source = refs[:3], refs[3]
    out_ref, partial_ref, outer_ref, weight_ref, index_ref = refs[4:9]
    held, near, sigma, table, product, staged, held_sem, near_sem, outer_sem, sigma_sem = refs[9:]
    _, energies, cell_count, _, _ = sigma_source.shape
    slots = kept_ref.shape[1]
    last = cell_count - 1
    steps = (cell_count - 2) * energies
    diag, lower, upper = sources

    def held_copies(step):
        position, energy = step // energies, step % energies
        return [
            pltpu.make_async_copy(
                source.at[:, energy, position + 1],
                held.at[term, :, energy, position],
                held_sem.at[term, step],
            )
            for term, source in enumerate(sources)
        ]

    def sigma_copy(energy):
        return pltpu.make_async_copy(
            sigma_source.at[:, energy], sigma.at[:, energy], sigma_sem.at[energy]
        )

    def near_copies(edge, energy):
        return [
            pltpu.make_async_copy(
                source.at[:, energy, edge * last],
                near.at[term, :, energy, edge],
                near_sem.at[term, energy, edge],
            )
            for term, source in enumerate((diag, (upper, lower)[edge]))
        ]

    def outer_copy(edge, energy):
        return pltpu.make_async_copy(
            (lower, upper)[edge].at[:, energy, edge * last],
            outer_ref.at[:, energy, edge],
            outer_sem.at[energy, edge],
        )

    ahead = min(energies, steps)
    for step in range(ahead):
        sigma_copy(step % energies).start()
        for copy in held_copies(step):
            copy.start()
    live = jnp.int32(0)
    for cell in range(cell_count):
        live = live + count_ref[cell]
    index = jnp.int32(0)
    for size in sizes[:-1]:
        index = index + jnp.where(live > size, 1, 0)
    index_ref[0] = index
    fill_mixing(screened_ref, weight_ref, table)

    def pair_of(ref, energy, spot):
        return ref[0, energy, spot], ref[1, energy, spot]

    def inside(step, _):
        position, energy = step // energies, step % energies
        cell = position + 1

        @pl.when(step + ahead < steps)
        def _():
            for copy in held_copies(step + ahead):
                copy.start()

        @pl.when(step == ahead - 1)
        def _():
            for edge in range(2):
                for other in range(energies):
                    for copy in near_copies(edge, other):
                        copy.start()
                    outer_copy(edge, other).start()

        @pl.when(position == 0)
        def _():
            sigma_copy(energy).wait()

        for copy in held_copies(step):
            copy.wait()
        products = sandwiches(
            [pair_of(held.at[term], energy, position) for term in range(3)],
            [pair_of(sigma, energy, other) for other in (cell, cell - 1, cell + 1)],
        )
        stage_slots(products, kept_ref, cell, energy, devices, out_ref.shape[2], product, staged)

        @pl.when(energy == energies - 1)
        def _():
            base = slot_base(count_ref, order, position)
            for slot in range(slots):
                out_ref[:, base + slot] = slot_tiles(staged, slot, out_ref)

        return 0

    lax.fori_loop(0, steps, inside, 0)
    for edge, cells in enumerate(((0, 1), (last, last - 1))):

        def beside(energy, _, edge=edge, cells=cells):
            for copy in near_copies(edge, energy):
                copy.wait()
            partial_ref[edge, energy] = sandwiches(
                [pair_of(near.at[term], energy, edge) for term in range(2)],
                [pair_of(sigma, energy, cell) for cell in cells],
            )
            return 0

        lax.fori_loop(0, energies, beside, 0)
    for edge in range(2):
        for energy in range(energies):
            outer_copy(edge, energy).wait()


def edge_kernel(
    order, kept_ref, count_ref, partial_ref, outer_ref, halo_first, halo_second, earlier, *refs
):
    *outs, out_ref, product, staged = refs
    _, energies, edge_count, _, _ = outer_ref.shape
    devices, total, tile_rows, _ = out_ref.shape
    ready = min(earlier.shape[1], total)
    out_ref[:, :ready] = earlier[:, :ready]
    odd = lax.axis_index("cell") % 2
    for edge, halo in ((1 - odd, halo_first), (odd, halo_second)):
        position = len(order) - edge_count + edge
        cell = edge * (len(order) - 1)
        base = slot_base(count_ref, order, position)
        for energy in range(energies):
            products = partial_ref[edge, energy] + sandwiches(
                [(outer_ref[0, energy, edge], outer_ref[1, energy, edge])],
                [(halo[0, energy, 0], halo[1, energy, 0])],
            )
            stage_slots(
                products, kept_ref, cell, energy, devices, tile_rows, product.at[energy], staged
            )
        for slot in range(kept_ref.shape[1]):

            @pl.when(slot < count_ref[cell])
            def _(slot=slot, base=base):
                out_ref[:, base + slot] = slot_tiles(staged, slot, out_ref)

    for bits, out in zip(partners(devices), outs):
        out[...] = out_ref[partner_of(bits, devices)]


SCALARS = pl.BlockSpec(memory_space=pltpu.SMEM)
VECTORS = pl.BlockSpec(memory_space=pltpu.VMEM)
STAYING = pl.BlockSpec(memory_space=pltpu.HBM)


def cost_of(places, energies, size):
    return pl.CostEstimate(
        flops=places * energies * 48 * size**3,
        bytes_accessed=places * energies * 6 * size * size * 4,
        transcendentals=0,
    )


def fill_scratch(size, slots, rows):
    return [
        pltpu.VMEM(((size // SUB) ** 2, LANES, LANES), jnp.float32),
        pltpu.VMEM((slots, rows, LANES), jnp.float32),
    ]


def local_part(blocks, screened, kept, kept_count, devices, sizes):
    _, energies, cells, size, _ = blocks[0].shape
    slots = kept.shape[1]
    share = PAIRS // devices
    tile_rows = energies * 2 * share
    rows = 2 * screened.shape[2] // 2 * share
    places = cells - 2
    wide = 2 * size

    def bfloat(*shape):
        return jax.ShapeDtypeStruct(shape, jnp.bfloat16)

    return pl.pallas_call(
        partial(local_kernel, packing_order(cells), devices, sizes),
        in_specs=[SCALARS, SCALARS, VECTORS] + [STAYING] * 4,
        out_specs=[VECTORS] * 4 + [SCALARS],
        out_shape=[
            bfloat(devices, places * slots, tile_rows, LANES),
            jax.ShapeDtypeStruct((2, energies, wide, wide), jnp.float32),
            bfloat(2, energies, 2, size, size),
            bfloat(cells, rows, rows),
            jax.ShapeDtypeStruct((1,), jnp.int32),
        ],
        scratch_shapes=[
            pltpu.VMEM((3, 2, energies, places, size, size), jnp.bfloat16),
            pltpu.VMEM((2, 2, energies, 2, size, size), jnp.bfloat16),
            pltpu.VMEM((2, energies, cells, size, size), jnp.bfloat16),
            pltpu.VMEM((cells, 2 * share, 2 * rows), jnp.float32),
        ]
        + fill_scratch(size, slots, devices * tile_rows)
        + [
            pltpu.SemaphoreType.DMA((3, energies * places)),
            pltpu.SemaphoreType.DMA((2, energies, 2)),
            pltpu.SemaphoreType.DMA((energies, 2)),
            pltpu.SemaphoreType.DMA((energies,)),
        ],
        compiler_params=pltpu.CompilerParams(vmem_limit_bytes=55 << 20),
        cost_estimate=cost_of(cells, energies, size),
    )(kept, kept_count, screened, *blocks)


def edges(total, partial_sum, outer, halo, earlier, kept, kept_count):
    _, energies, _, size, _ = outer.shape
    devices, _, tile_rows, _ = earlier.shape
    return pl.pallas_call(
        partial(edge_kernel, packing_order(kept.shape[0])),
        in_specs=[SCALARS, SCALARS] + [VECTORS] * 5,
        out_specs=[VECTORS] * devices,
        out_shape=[jax.ShapeDtypeStruct((total, tile_rows, LANES), jnp.bfloat16)] * devices,
        scratch_shapes=[pltpu.VMEM((devices, total, tile_rows, LANES), jnp.bfloat16)]
        + [
            pltpu.VMEM((energies, (size // SUB) ** 2, LANES, LANES), jnp.float32),
            pltpu.VMEM((kept.shape[1], devices * tile_rows, LANES), jnp.float32),
        ],
        compiler_params=pltpu.CompilerParams(vmem_limit_bytes=32 << 20),
        cost_estimate=cost_of(1, energies, size),
    )(kept, kept_count, partial_sum, outer, *halo, earlier)


def border_kernel(sigma, out, sem):
    cell = jnp.where(lax.axis_index("cell") % 2 == 1, 0, sigma.shape[2] - 1)
    copy = pltpu.make_async_copy(sigma.at[:, :, pl.ds(cell, 1)], out, sem)
    copy.start()
    copy.wait()


def border(sigma):
    return pl.pallas_call(
        border_kernel,
        in_specs=[STAYING],
        out_specs=VECTORS,
        out_shape=jax.ShapeDtypeStruct(sigma.shape[:2] + (1,) + sigma.shape[3:], sigma.dtype),
        scratch_shapes=[pltpu.SemaphoreType.DMA],
        compiler_params=pltpu.CompilerParams(vmem_limit_bytes=60 << 20),
    )(sigma)


def fill_mixing(screened_ref, weight_ref, table):
    _, cells, doubled = screened_ref.shape
    _, rows, lane_count = table.shape
    total, share = doubled // 2, rows // 2
    shape = (2 * doubled, lane_count)
    source = lax.broadcasted_iota(jnp.int32, shape, 0)
    lane = lax.broadcasted_iota(jnp.int32, shape, 1)
    offset = 2 * total - 2 - lane // rows
    part = (lane // share) % 2
    spot = lane % share
    both = jnp.concatenate([screened_ref[0], screened_ref[1]], axis=1)
    for row in range(rows):
        own_part, own_spot = row // share, row % share
        wanted = jnp.where(part == own_part, 0, doubled) + offset
        sign = jnp.where(part > own_part, -1.0, 1.0)
        pick = jnp.where((source == wanted) & (spot == own_spot) & (offset >= 0), sign, 0.0)
        table[:, row, :] = jnp.dot(
            both, pick.astype(jnp.bfloat16), preferred_element_type=jnp.float32
        )
    size = weight_ref.shape[1]
    for cell in range(cells):
        for energy in range(total):
            start = (total - 1 - energy) * rows
            weight_ref[cell, energy * rows : (energy + 1) * rows, :] = table[
                cell, :, start : start + size
            ].astype(jnp.bfloat16)


def mix_kernel(order, count_ref, weight_ref, *refs):
    parts, outs, x_ref, y_ref = refs[: len(refs) // 2 - 1], refs[len(refs) // 2 - 1 : -2], *refs[-2:]
    devices, total, tile_rows, _ = x_ref.shape
    for bits, part in zip(partners(devices), parts):
        x_ref[partner_of(bits, devices)] = part[...]
    ends = []
    end = jnp.int32(0)
    for cell in order[:-1]:
        end = end + count_ref[cell]
        ends.append(end)
    for slot in range(total):
        cell = jnp.int32(order[-1])
        for name, end in reversed(list(zip(order, ends))):
            cell = jnp.where(slot < end, name, cell)
        entries = x_ref[:, slot].reshape(devices * tile_rows, LANES)
        mixed = jnp.dot(weight_ref[cell], entries, preferred_element_type=jnp.float32)
        y_ref[:, slot] = mixed.astype(jnp.bfloat16).reshape(devices, tile_rows, LANES)
    for bits, out in zip(partners(devices), outs):
        out[...] = y_ref[partner_of(bits, devices)]


def mix(parts, weights, kept_count):
    devices = len(parts)
    return pl.pallas_call(
        partial(mix_kernel, packing_order(kept_count.shape[0])),
        in_specs=[SCALARS, VECTORS] + [VECTORS] * devices,
        out_specs=[VECTORS] * devices,
        out_shape=[jax.ShapeDtypeStruct(parts[0].shape, jnp.bfloat16)] * devices,
        scratch_shapes=[pltpu.VMEM((devices, *parts[0].shape), jnp.bfloat16)] * 2,
        compiler_params=pltpu.CompilerParams(vmem_limit_bytes=16 << 20),
    )(kept_count, weights, *parts)


def unpack_kernel(order, count_ref, *refs):
    *parts, out_ref, rows, cells_out, sems = refs
    devices = len(parts)
    total, tile_rows, _ = parts[0].shape
    pitch = tile_rows + 1
    _, energies, cell_count, slots, _ = out_ref.shape
    share = PAIRS // devices
    copies = []
    for position, cell in enumerate(order):
        base = slot_base(count_ref, order, position)
        held = rows.at[position % 2]
        for slot in range(slots):
            number = jnp.minimum(base + slot, total - 1)
            start = slot * pitch
            for bits, part in zip(partners(devices), parts):
                held[partner_of(bits, devices), start : start + tile_rows, :] = part[
                    number
                ].astype(jnp.float32)
        live = lax.broadcasted_iota(jnp.int32, (slots, LANES), 0) < count_ref[cell]
        for part in range(2):
            for energy in range(energies):
                for index in range(PAIRS):
                    row = (energy * 2 + part) * share + index // devices
                    entries = held[index % devices, pl.ds(row, slots, stride=pitch), :]
                    cells_out[part, energy, cell, :, index * LANES : (index + 1) * LANES] = (
                        jnp.where(live, entries, 0.0).astype(jnp.bfloat16)
                    )
        copy = pltpu.make_async_copy(cells_out.at[:, :, cell], out_ref.at[:, :, cell], sems.at[cell])
        copy.start()
        copies.append(copy)
    for copy in copies:
        copy.wait()


def unpack(parts, kept_count, energies, slots):
    devices = len(parts)
    cells = kept_count.shape[0]
    shape = (2, energies, cells, slots, SUB * SUB)
    return pl.pallas_call(
        partial(unpack_kernel, packing_order(cells)),
        in_specs=[SCALARS] + [VECTORS] * devices,
        out_specs=STAYING,
        out_shape=pltpu.HBM(shape, jnp.bfloat16),
        scratch_shapes=[
            pltpu.VMEM((2, devices, slots * (parts[0].shape[1] + 1), LANES), jnp.float32),
            pltpu.VMEM(shape, jnp.bfloat16),
            pltpu.SemaphoreType.DMA((cells,)),
        ],
        compiler_params=pltpu.CompilerParams(vmem_limit_bytes=16 << 20),
    )(kept_count, *parts)


def per_device(diag, lower, upper, sigma, screened, kept, kept_count):
    count = lax.axis_size("cell")
    devices = lax.axis_size("energy")
    outward = lax.axis_index("cell") % 2 * (sigma.shape[2] - 1)
    edge_cell = lax.dynamic_slice_in_dim(sigma, outward, 1, axis=2)

    def swap(block, start):
        pairs = [(low, low + 1) for low in range(start, count - 1, 2)]
        return lax.ppermute(block, "cell", pairs + [(high, low) for low, high in pairs])

    halo = swap(border(sigma), 0), swap(edge_cell, 1)
    energies, slots = sigma.shape[1], kept.shape[1]
    full = kept.shape[0] * slots
    sizes = [full * eighths // 8 for eighths in (4, 5, 6, 7, 8)]
    earlier, partial_sum, outer, weights, index = local_part(
        (diag, lower, upper, sigma), screened, kept, kept_count, devices, sizes
    )

    def with_slots(total, partial_sum, outer, halo, earlier, weights, kept, kept_count):
        parts = edges(total, partial_sum, outer, halo, earlier, kept, kept_count)
        mixed = mix(exchange(parts), weights, kept_count)
        return unpack(exchange(mixed), kept_count, energies, slots)

    return lax.switch(
        index[0],
        [partial(with_slots, size) for size in sizes],
        partial_sum, outer, halo, earlier, weights, kept, kept_count,
    )


def solution(mesh):
    placed = (
        P(None, "energy", "cell", None, None),
        P(None, "energy", "cell", None, None),
        P(None, "energy", "cell", None, None),
        P(None, "energy", "cell", None, None),
        P(None, "cell", None),
        P("cell", None),
        P("cell"),
    )
    return jax.shard_map(
        per_device,
        mesh=mesh,
        in_specs=placed,
        out_specs=P(None, "energy", "cell", None, None),
        check_vma=False,
    )
```

```python
from functools import partial

import jax
import jax.numpy as jnp
from jax import lax
from jax.experimental import pallas as pl
from jax.experimental.pallas import tpu as pltpu
from jax.sharding import PartitionSpec as P

SUB = 64
LANES = 2 * SUB
PAIRS = SUB // 2
STEP = 8


def pairwise(devices):
    return devices <= STEP and devices & (devices - 1) == 0


def partners(devices):
    if not pairwise(devices):
        return list(range(devices))
    others = sorted(
        range(1, devices), key=lambda bits: (-bin(bits >> 1).count("1"), bits & 1, bits)
    )
    return [0] + others


def partner_of(bits, devices):
    if not pairwise(devices):
        return bits
    return lax.axis_index("energy") ^ bits


def exchange(parts):
    devices = len(parts)
    if not pairwise(devices):
        sent = lax.all_to_all(jnp.stack(parts), "energy", split_axis=0, concat_axis=0, tiled=True)
        return [sent[index] for index in range(devices)]
    return [parts[0]] + [
        lax.ppermute(part, "energy", [(source, source ^ bits) for source in range(devices)])
        for bits, part in zip(partners(devices)[1:], parts[1:])
    ]


def packing_order(cell_count):
    interior = list(range(1, cell_count - 1))
    return interior + [0, cell_count - 1] if cell_count > 1 else [0]


def slot_base(count_ref, order, position):
    base = jnp.int32(0)
    for place, cell in enumerate(order[:-1]):
        base = base + jnp.where(place < position, count_ref[cell], 0)
    return base


def inner_products(factor, middle_r, middle_i):
    row = jnp.concatenate([factor[0], factor[1]], axis=1)
    real_part = jnp.dot(
        row, jnp.concatenate([middle_r, -middle_i], axis=0), preferred_element_type=jnp.float32
    )
    imag_part = jnp.dot(
        row, jnp.concatenate([middle_i, middle_r], axis=0), preferred_element_type=jnp.float32
    )
    return by_strips(real_part.astype(jnp.bfloat16), imag_part.astype(jnp.bfloat16))


def by_strips(real_part, imag_part):
    pieces = []
    for start in range(0, real_part.shape[0], SUB):
        pieces += [real_part[start : start + SUB], imag_part[start : start + SUB]]
    return jnp.concatenate(pieces, axis=0)


def paired_rows(product_ref, number, group):
    def rows(half, odd):
        start = half * SUB + group * 2 * STEP + odd
        return product_ref[number, pl.ds(start, STEP, stride=2), :]

    left = lax.broadcasted_iota(jnp.int32, (STEP, LANES), 1) < SUB
    top_even, top_odd = rows(0, 0), rows(0, 1)
    low_even, low_odd = rows(1, 0), rows(1, 1)
    real_part = jnp.where(left, top_even, low_odd) + pltpu.roll(
        jnp.where(left, top_odd, low_even), SUB, 1
    )
    imag_part = jnp.where(left, low_even, -top_odd) + pltpu.roll(
        jnp.where(left, low_odd, -top_even), SUB, 1
    )
    return real_part, imag_part


def sandwiches(factors, middles):
    inner = jnp.concatenate(
        [inner_products(factor, *middle) for factor, middle in zip(factors, middles)], axis=1
    )
    return lax.dot_general(
        inner,
        jnp.concatenate([by_strips(*factor) for factor in factors], axis=1),
        (((1,), (1,)), ((), ())),
        preferred_element_type=jnp.float32,
    )


def stage_slots(products, kept_ref, cell, energy, devices, tile_rows, product, staged):
    per_side = products.shape[0] // LANES
    share = PAIRS // devices
    for top in range(per_side):
        for side in range(per_side):
            product[top * per_side + side] = products[
                top * LANES : (top + 1) * LANES, side * LANES : (side + 1) * LANES
            ]
    for slot in range(kept_ref.shape[1]):
        number = kept_ref[cell, slot]
        for group in range(PAIRS // STEP):
            pair = paired_rows(product, number, group)
            device = (group * STEP) % devices
            for part in range(2):
                row = (energy * 2 + part) * share + group * STEP // devices
                start = device * tile_rows + row
                staged[slot, pl.ds(start, STEP, stride=tile_rows), :] = pair[part]


def slot_tiles(staged, slot, out_ref):
    devices, _, tile_rows, _ = out_ref.shape
    return staged[slot].reshape(devices, tile_rows, LANES).astype(jnp.bfloat16)


def local_kernel(order, devices, sizes, kept_ref, count_ref, screened_ref, *refs):
    sources, sigma_source = refs[:3], refs[3]
    out_ref, partial_ref, outer_ref, weight_ref, index_ref = refs[4:9]
    held, near, sigma, table, product, staged, held_sem, near_sem, outer_sem, sigma_sem = refs[9:]
    _, energies, cell_count, _, _ = sigma_source.shape
    slots = kept_ref.shape[1]
    last = cell_count - 1
    steps = (cell_count - 2) * energies
    diag, lower, upper = sources

    def held_copies(step):
        position, energy = step // energies, step % energies
        return [
            pltpu.make_async_copy(
                source.at[:, energy, position + 1],
                held.at[term, :, energy, position],
                held_sem.at[term, step],
            )
            for term, source in enumerate(sources)
        ]

    def sigma_copy(energy):
        return pltpu.make_async_copy(
            sigma_source.at[:, energy], sigma.at[:, energy], sigma_sem.at[energy]
        )

    def near_copies(edge, energy):
        return [
            pltpu.make_async_copy(
                source.at[:, energy, edge * last],
                near.at[term, :, energy, edge],
                near_sem.at[term, energy, edge],
            )
            for term, source in enumerate((diag, (upper, lower)[edge]))
        ]

    def outer_copy(edge, energy):
        return pltpu.make_async_copy(
            (lower, upper)[edge].at[:, energy, edge * last],
            outer_ref.at[:, energy, edge],
            outer_sem.at[energy, edge],
        )

    ahead = min(energies, steps)
    for step in range(ahead):
        sigma_copy(step % energies).start()
        for copy in held_copies(step):
            copy.start()
    live = jnp.int32(0)
    for cell in range(cell_count):
        live = live + count_ref[cell]
    index = jnp.int32(0)
    for size in sizes[:-1]:
        index = index + jnp.where(live > size, 1, 0)
    index_ref[0] = index
    fill_mixing(screened_ref, weight_ref, table)

    def pair_of(ref, energy, spot):
        return ref[0, energy, spot], ref[1, energy, spot]

    def inside(step, _):
        position, energy = step // energies, step % energies
        cell = position + 1

        @pl.when(step + ahead < steps)
        def _():
            for copy in held_copies(step + ahead):
                copy.start()

        @pl.when(step == ahead - 1)
        def _():
            for edge in range(2):
                for other in range(energies):
                    for copy in near_copies(edge, other):
                        copy.start()
                    outer_copy(edge, other).start()

        @pl.when(position == 0)
        def _():
            sigma_copy(energy).wait()

        for copy in held_copies(step):
            copy.wait()
        products = sandwiches(
            [pair_of(held.at[term], energy, position) for term in range(3)],
            [pair_of(sigma, energy, other) for other in (cell, cell - 1, cell + 1)],
        )
        stage_slots(products, kept_ref, cell, energy, devices, out_ref.shape[2], product, staged)

        @pl.when(energy == energies - 1)
        def _():
            base = slot_base(count_ref, order, position)
            for slot in range(slots):
                out_ref[:, base + slot] = slot_tiles(staged, slot, out_ref)

        return 0

    lax.fori_loop(0, steps, inside, 0)
    for edge, cells in enumerate(((0, 1), (last, last - 1))):

        def beside(energy, _, edge=edge, cells=cells):
            for copy in near_copies(edge, energy):
                copy.wait()
            partial_ref[edge, energy] = sandwiches(
                [pair_of(near.at[term], energy, edge) for term in range(2)],
                [pair_of(sigma, energy, cell) for cell in cells],
            )
            return 0

        lax.fori_loop(0, energies, beside, 0)
    for edge in range(2):
        for energy in range(energies):
            outer_copy(edge, energy).wait()


def edge_kernel(
    order, kept_ref, count_ref, partial_ref, outer_ref, halo_first, halo_second, earlier, *refs
):
    *outs, out_ref, product, staged = refs
    _, energies, edge_count, _, _ = outer_ref.shape
    devices, total, tile_rows, _ = out_ref.shape
    ready = min(earlier.shape[1], total)
    out_ref[:, :ready] = earlier[:, :ready]
    odd = lax.axis_index("cell") % 2
    for edge, halo in ((1 - odd, halo_first), (odd, halo_second)):
        position = len(order) - edge_count + edge
        cell = edge * (len(order) - 1)
        base = slot_base(count_ref, order, position)
        for energy in range(energies):
            products = partial_ref[edge, energy] + sandwiches(
                [(outer_ref[0, energy, edge], outer_ref[1, energy, edge])],
                [(halo[0, energy, 0], halo[1, energy, 0])],
            )
            stage_slots(
                products, kept_ref, cell, energy, devices, tile_rows, product.at[energy], staged
            )
        for slot in range(kept_ref.shape[1]):

            @pl.when(slot < count_ref[cell])
            def _(slot=slot, base=base):
                out_ref[:, base + slot] = slot_tiles(staged, slot, out_ref)

    for bits, out in zip(partners(devices), outs):
        out[...] = out_ref[partner_of(bits, devices)]


SCALARS = pl.BlockSpec(memory_space=pltpu.SMEM)
VECTORS = pl.BlockSpec(memory_space=pltpu.VMEM)
STAYING = pl.BlockSpec(memory_space=pltpu.HBM)


def cost_of(places, energies, size):
    return pl.CostEstimate(
        flops=places * energies * 48 * size**3,
        bytes_accessed=places * energies * 6 * size * size * 4,
        transcendentals=0,
    )


def fill_scratch(size, slots, rows):
    return [
        pltpu.VMEM(((size // SUB) ** 2, LANES, LANES), jnp.float32),
        pltpu.VMEM((slots, rows, LANES), jnp.float32),
    ]


def local_part(blocks, screened, kept, kept_count, devices, sizes):
    _, energies, cells, size, _ = blocks[0].shape
    slots = kept.shape[1]
    share = PAIRS // devices
    tile_rows = energies * 2 * share
    rows = 2 * screened.shape[2] // 2 * share
    places = cells - 2
    wide = 2 * size

    def bfloat(*shape):
        return jax.ShapeDtypeStruct(shape, jnp.bfloat16)

    return pl.pallas_call(
        partial(local_kernel, packing_order(cells), devices, sizes),
        in_specs=[SCALARS, SCALARS, VECTORS] + [STAYING] * 4,
        out_specs=[VECTORS] * 4 + [SCALARS],
        out_shape=[
            bfloat(devices, places * slots, tile_rows, LANES),
            jax.ShapeDtypeStruct((2, energies, wide, wide), jnp.float32),
            bfloat(2, energies, 2, size, size),
            bfloat(cells, rows, rows),
            jax.ShapeDtypeStruct((1,), jnp.int32),
        ],
        scratch_shapes=[
            pltpu.VMEM((3, 2, energies, places, size, size), jnp.bfloat16),
            pltpu.VMEM((2, 2, energies, 2, size, size), jnp.bfloat16),
            pltpu.VMEM((2, energies, cells, size, size), jnp.bfloat16),
            pltpu.VMEM((cells, 2 * share, 2 * rows), jnp.float32),
        ]
        + fill_scratch(size, slots, devices * tile_rows)
        + [
            pltpu.SemaphoreType.DMA((3, energies * places)),
            pltpu.SemaphoreType.DMA((2, energies, 2)),
            pltpu.SemaphoreType.DMA((energies, 2)),
            pltpu.SemaphoreType.DMA((energies,)),
        ],
        compiler_params=pltpu.CompilerParams(vmem_limit_bytes=55 << 20),
        cost_estimate=cost_of(cells, energies, size),
    )(kept, kept_count, screened, *blocks)


def edges(total, partial_sum, outer, halo, earlier, kept, kept_count):
    _, energies, _, size, _ = outer.shape
    devices, _, tile_rows, _ = earlier.shape
    return pl.pallas_call(
        partial(edge_kernel, packing_order(kept.shape[0])),
        in_specs=[SCALARS, SCALARS] + [VECTORS] * 5,
        out_specs=[VECTORS] * devices,
        out_shape=[jax.ShapeDtypeStruct((total, tile_rows, LANES), jnp.bfloat16)] * devices,
        scratch_shapes=[pltpu.VMEM((devices, total, tile_rows, LANES), jnp.bfloat16)]
        + [
            pltpu.VMEM((energies, (size // SUB) ** 2, LANES, LANES), jnp.float32),
            pltpu.VMEM((kept.shape[1], devices * tile_rows, LANES), jnp.float32),
        ],
        compiler_params=pltpu.CompilerParams(vmem_limit_bytes=32 << 20),
        cost_estimate=cost_of(1, energies, size),
    )(kept, kept_count, partial_sum, outer, *halo, earlier)


def fill_mixing(screened_ref, weight_ref, table):
    _, cells, doubled = screened_ref.shape
    _, rows, lane_count = table.shape
    total, share = doubled // 2, rows // 2
    shape = (2 * doubled, lane_count)
    source = lax.broadcasted_iota(jnp.int32, shape, 0)
    lane = lax.broadcasted_iota(jnp.int32, shape, 1)
    offset = 2 * total - 2 - lane // rows
    part = (lane // share) % 2
    spot = lane % share
    both = jnp.concatenate([screened_ref[0], screened_ref[1]], axis=1)
    for row in range(rows):
        own_part, own_spot = row // share, row % share
        wanted = jnp.where(part == own_part, 0, doubled) + offset
        sign = jnp.where(part > own_part, -1.0, 1.0)
        pick = jnp.where((source == wanted) & (spot == own_spot) & (offset >= 0), sign, 0.0)
        table[:, row, :] = jnp.dot(
            both, pick.astype(jnp.bfloat16), preferred_element_type=jnp.float32
        )
    size = weight_ref.shape[1]
    for cell in range(cells):
        for energy in range(total):
            start = (total - 1 - energy) * rows
            weight_ref[cell, energy * rows : (energy + 1) * rows, :] = table[
                cell, :, start : start + size
            ].astype(jnp.bfloat16)


def mix_kernel(order, count_ref, weight_ref, *refs):
    parts, outs, x_ref, y_ref = refs[: len(refs) // 2 - 1], refs[len(refs) // 2 - 1 : -2], *refs[-2:]
    devices, total, tile_rows, _ = x_ref.shape
    for bits, part in zip(partners(devices), parts):
        x_ref[partner_of(bits, devices)] = part[...]
    ends = []
    end = jnp.int32(0)
    for cell in order[:-1]:
        end = end + count_ref[cell]
        ends.append(end)
    for slot in range(total):
        cell = jnp.int32(order[-1])
        for name, end in reversed(list(zip(order, ends))):
            cell = jnp.where(slot < end, name, cell)
        entries = x_ref[:, slot].reshape(devices * tile_rows, LANES)
        mixed = jnp.dot(weight_ref[cell], entries, preferred_element_type=jnp.float32)
        y_ref[:, slot] = mixed.astype(jnp.bfloat16).reshape(devices, tile_rows, LANES)
    for bits, out in zip(partners(devices), outs):
        out[...] = y_ref[partner_of(bits, devices)]


def mix(parts, weights, kept_count):
    devices = len(parts)
    return pl.pallas_call(
        partial(mix_kernel, packing_order(kept_count.shape[0])),
        in_specs=[SCALARS, VECTORS] + [VECTORS] * devices,
        out_specs=[VECTORS] * devices,
        out_shape=[jax.ShapeDtypeStruct(parts[0].shape, jnp.bfloat16)] * devices,
        scratch_shapes=[pltpu.VMEM((devices, *parts[0].shape), jnp.bfloat16)] * 2,
        compiler_params=pltpu.CompilerParams(vmem_limit_bytes=16 << 20),
    )(kept_count, weights, *parts)


def unpack_kernel(order, count_ref, *refs):
    *parts, out_ref, rows, cells_out, sems = refs
    devices = len(parts)
    total, tile_rows, _ = parts[0].shape
    pitch = tile_rows + 1
    _, energies, cell_count, slots, _ = out_ref.shape
    share = PAIRS // devices
    copies = []
    for position, cell in enumerate(order):
        base = slot_base(count_ref, order, position)
        held = rows.at[position % 2]
        for slot in range(slots):
            number = jnp.minimum(base + slot, total - 1)
            start = slot * pitch
            for bits, part in zip(partners(devices), parts):
                held[partner_of(bits, devices), start : start + tile_rows, :] = part[
                    number
                ].astype(jnp.float32)
        live = lax.broadcasted_iota(jnp.int32, (slots, LANES), 0) < count_ref[cell]
        for part in range(2):
            for energy in range(energies):
                for index in range(PAIRS):
                    row = (energy * 2 + part) * share + index // devices
                    entries = held[index % devices, pl.ds(row, slots, stride=pitch), :]
                    cells_out[part, energy, cell, :, index * LANES : (index + 1) * LANES] = (
                        jnp.where(live, entries, 0.0).astype(jnp.bfloat16)
                    )
        copy = pltpu.make_async_copy(cells_out.at[:, :, cell], out_ref.at[:, :, cell], sems.at[cell])
        copy.start()
        copies.append(copy)
    for copy in copies:
        copy.wait()


def unpack(parts, kept_count, energies, slots):
    devices = len(parts)
    cells = kept_count.shape[0]
    shape = (2, energies, cells, slots, SUB * SUB)
    return pl.pallas_call(
        partial(unpack_kernel, packing_order(cells)),
        in_specs=[SCALARS] + [VECTORS] * devices,
        out_specs=STAYING,
        out_shape=pltpu.HBM(shape, jnp.bfloat16),
        scratch_shapes=[
            pltpu.VMEM((2, devices, slots * (parts[0].shape[1] + 1), LANES), jnp.float32),
            pltpu.VMEM(shape, jnp.bfloat16),
            pltpu.SemaphoreType.DMA((cells,)),
        ],
        compiler_params=pltpu.CompilerParams(vmem_limit_bytes=16 << 20),
    )(kept_count, *parts)


def per_device(diag, lower, upper, sigma, screened, kept, kept_count):
    count = lax.axis_size("cell")
    devices = lax.axis_size("energy")
    odd = lax.axis_index("cell") % 2 == 1
    first, last = sigma[:, :, :1], sigma[:, :, -1:]

    def swap(block, start):
        pairs = [(low, low + 1) for low in range(start, count - 1, 2)]
        return lax.ppermute(block, "cell", pairs + [(high, low) for low, high in pairs])

    halo = swap(jnp.where(odd, first, last), 0), swap(jnp.where(odd, last, first), 1)
    energies, slots = sigma.shape[1], kept.shape[1]
    full = kept.shape[0] * slots
    sizes = [full * eighths // 8 for eighths in (4, 5, 6, 7, 8)]
    earlier, partial_sum, outer, weights, index = local_part(
        (diag, lower, upper, sigma), screened, kept, kept_count, devices, sizes
    )

    def with_slots(total, partial_sum, outer, halo, earlier, weights, kept, kept_count):
        parts = edges(total, partial_sum, outer, halo, earlier, kept, kept_count)
        mixed = mix(exchange(parts), weights, kept_count)
        return unpack(exchange(mixed), kept_count, energies, slots)

    return lax.switch(
        index[0],
        [partial(with_slots, size) for size in sizes],
        partial_sum, outer, halo, earlier, weights, kept, kept_count,
    )


def solution(mesh):
    placed = (
        P(None, "energy", "cell", None, None),
        P(None, "energy", "cell", None, None),
        P(None, "energy", "cell", None, None),
        P(None, "energy", "cell", None, None),
        P(None, "cell", None),
        P("cell", None),
        P("cell"),
    )
    return jax.shard_map(
        per_device,
        mesh=mesh,
        in_specs=placed,
        out_specs=P(None, "energy", "cell", None, None),
        check_vma=False,
    )
```
